32 devices in a mesh: blk: 8 (over y, x, core), grp: 4 (over z).
Axes of the slice: x: 2, y: 2, z: 4, core: 2. Of those that a mesh axis runs over, the one named last changes fastest.
Arguments:
- inverse: bfloat16 [2, 8, 1024, 1024], P(None, 'blk', 'grp'), may hold values from -0.0034375 to 0.1734375
- excite: bfloat16 [2, 8, 1024, 128], P(None, 'blk'), may hold values from -0.125 to 0.125
- coordinates: int32 [3, 8, 1024], replicated, may hold values from 0 to 31, as said below
- block_of_slot: int32 [8], replicated, may hold values from 0 to 7, each once
- panel_order: int32 [8], replicated, may hold values from 0 to 7, each once
Outputs:
- reduced: float32 [2, 1024, 1024], P(None, 'blk', 'grp')
- schur: float32 [2, 1024, 1024], P(None, 'blk', 'grp')
The draws below stay inside these ranges and needn't reach their ends.
Inputs may be any that keep to these rules, and one draw needn't show every extreme that they name: `coordinates`: components 0 and 1 lie in 0 to 31, component 2 in 0 to 15. No two unknowns of any blocks share a lattice point. `block_of_slot`: slot s is the (s mod 1)-th block of index s // 1 of blk; every block number appears once. `panel_order`: every block number appears once; the first 2 are eliminated in that order, without pivoting.
All inputs are finite; a program needn't handle non-finite values.
Results may differ from the reference program's by a relative error of at most 0.0055.
Values may be sent and summed in bfloat16 or wider, within the bound.
A program may use at most 64 MiB of HBM per device.

```python
import math
import jax
import jax.numpy as jnp
from jax import lax

UNK = 1024
NCBF = 128
PANELS = 2
BLOCKS = 8
ORDER = 1024


def patch_shape():
    log_size = UNK.bit_length() - 1
    patch_width = 2 ** ((log_size + 1) // 2)
    return (patch_width, UNK // patch_width)


def draw_coordinates(key, part):
    base = jax.random.fold_in(key, 17)
    pick_key, order_key, flip_key = jax.random.split(base, 3)
    patch_width, patch_height = patch_shape()
    per_layer = 1024 // UNK
    across = 32 // patch_width
    positions = jnp.arange(BLOCKS, dtype=jnp.int32)
    choose = jax.random.randint(pick_key, (BLOCKS,), 0, 2).astype(jnp.int32)
    choose = jnp.where(positions == 0, 0, jnp.where(positions == BLOCKS - 1, 1, choose))
    slot_ids = 2 * positions + choose
    shuffle = jax.random.permutation(order_key, BLOCKS).astype(jnp.int32)
    placed = jnp.take(slot_ids, shuffle)
    layer_of = placed // per_layer
    patch_of = placed % per_layer
    start_x = patch_of % across * patch_width
    start_y = patch_of // across * patch_height
    mirror = jax.random.randint(flip_key, (2, BLOCKS, 1), 0, 2).astype(jnp.int32)
    unknown = jnp.arange(UNK, dtype=jnp.int32)
    inner_x = (unknown % patch_width)[None, :]
    inner_y = (unknown // patch_width)[None, :]
    first = start_x[:, None] + jnp.where(mirror[0] == 1, patch_width - 1 - inner_x, inner_x)
    second = start_y[:, None] + jnp.where(mirror[1] == 1, patch_height - 1 - inner_y, inner_y)
    third = jnp.broadcast_to(layer_of[:, None], (BLOCKS, UNK))
    return jnp.stack([first, second, third]).astype(jnp.int32)


def draw_excite(key, part):
    base = jax.random.fold_in(key, 29)
    keys = jax.random.split(base, 5)
    patch_width, patch_height = patch_shape()
    columns = (BLOCKS, 1, NCBF)
    radius = 0.7 * jnp.sqrt(jax.random.uniform(keys[0], columns, jnp.float32))
    heading = jax.random.uniform(keys[1], columns, jnp.float32, -math.pi, math.pi)
    offset = jax.random.uniform(keys[2], columns, jnp.float32, -math.pi, math.pi)
    level = jnp.exp(jax.random.uniform(keys[3], columns, jnp.float32, math.log(0.04), math.log(0.08)))
    rough = 1.0 + 0.5 * jax.random.uniform(keys[4], (BLOCKS, UNK, NCBF), jnp.float32, -1.0, 1.0)
    unknown = jnp.arange(UNK, dtype=jnp.int32)
    inner_x = (unknown % patch_width).astype(jnp.float32)[None, :, None]
    inner_y = (unknown // patch_width).astype(jnp.float32)[None, :, None]
    angle = radius * (jnp.cos(heading) * inner_x + jnp.sin(heading) * inner_y) + offset
    amplitude = level * rough
    return jnp.stack([amplitude * jnp.cos(angle), amplitude * jnp.sin(angle)]).astype(jnp.bfloat16)


def draw_inverse(key, part):
    base = jax.random.fold_in(key, 41)
    diag_key, noise_key = jax.random.split(base, 2)
    spread = 0.025 / math.sqrt(UNK)
    diagonal = jnp.exp(jax.random.uniform(diag_key, (BLOCKS, UNK, 1), jnp.float32, math.log(0.07), math.log(0.14)))
    noise = spread * jnp.clip(jax.random.normal(noise_key, (2, BLOCKS, UNK, UNK), jnp.float32), -4.0, 4.0)
    unknown = jnp.arange(UNK, dtype=jnp.int32)
    identity_mask = (unknown[:, None] == unknown[None, :]).astype(jnp.float32)
    real_part = diagonal * identity_mask[None] + noise[0]
    return jnp.stack([real_part, noise[1]]).astype(jnp.bfloat16)


def setup_inputs(seed: int = 0) -> dict:
    arg_keys = jax.random.split(jax.random.key(seed), 6)
    inverse = draw_inverse(jax.random.fold_in(arg_keys[5], 71), 0)
    excite = draw_excite(jax.random.fold_in(arg_keys[5], 71), 0)
    coordinates = draw_coordinates(jax.random.fold_in(arg_keys[5], 71), 0)
    block_of_slot = jax.random.permutation(arg_keys[3], BLOCKS).astype(jnp.int32)
    panel_order = jax.random.permutation(arg_keys[4], BLOCKS).astype(jnp.int32)
    return dict(inverse=inverse, excite=excite, coordinates=coordinates, block_of_slot=block_of_slot, panel_order=panel_order)


SELF_REAL = 12.0
SELF_IMAG = -3.0
COUPLE = 2.0
WAVE = 1.3

def green_tile(test_pos, basis_pos):
    squared = jnp.zeros((test_pos.shape[1], basis_pos.shape[1]), jnp.int32)
    for which in range(3):
        spacing = test_pos[which][:, None] - basis_pos[which][None, :]
        squared = squared + spacing * spacing
    coincide = squared == 0
    distance = jnp.sqrt(jnp.maximum(squared, 1).astype(jnp.float32))
    scaled = COUPLE / distance
    angle_term = WAVE * distance
    real_part = jnp.where(coincide, jnp.float32(SELF_REAL), scaled * jnp.cos(angle_term))
    imag_part = jnp.where(coincide, jnp.float32(SELF_IMAG), -scaled * jnp.sin(angle_term))
    return (real_part.astype(jnp.bfloat16), imag_part.astype(jnp.bfloat16))

def solve_pivot(pivot, right):
    top = jnp.concatenate([pivot[0], -pivot[1]], axis=1)
    lower = jnp.concatenate([pivot[1], pivot[0]], axis=1)
    real_form = jnp.concatenate([top, lower], axis=0)
    stacked = jnp.concatenate([right[0], right[1]], axis=0)
    answer = jnp.linalg.solve(real_form, stacked)
    return (answer[:NCBF], answer[NCBF:])

def reference(inverse, excite, coordinates, block_of_slot, panel_order):
    upper_bound = lax.Precision.HIGHEST
    inv_wide = inverse.astype(jnp.float32)
    exc_wide = excite.astype(jnp.float32)
    basis_real = jnp.einsum('sur,src->suc', inv_wide[0], exc_wide[0], precision=upper_bound) - jnp.einsum('sur,src->suc', inv_wide[1], exc_wide[1], precision=upper_bound)
    basis_imag = jnp.einsum('sur,src->suc', inv_wide[0], exc_wide[1], precision=upper_bound) + jnp.einsum('sur,src->suc', inv_wide[1], exc_wide[0], precision=upper_bound)
    basis = jnp.stack([basis_real, basis_imag]).astype(jnp.bfloat16)
    slot_of_block = jnp.argsort(block_of_slot).astype(jnp.int32)
    grouped_per_block = basis[:, slot_of_block].astype(jnp.float32)
    all_pos = coordinates.reshape(3, BLOCKS * UNK)

    def one_row(block_a):
        test_pos = coordinates[:, block_a]
        greens_function_real, greens_function_imaginary = green_tile(test_pos, all_pos)
        greens_function_real = greens_function_real.astype(jnp.float32).reshape(UNK, BLOCKS, UNK)
        greens_function_imaginary = greens_function_imaginary.astype(jnp.float32).reshape(UNK, BLOCKS, UNK)
        product_real = jnp.einsum('kpn,pnj->pkj', greens_function_real, grouped_per_block[0], precision=upper_bound) - jnp.einsum('kpn,pnj->pkj', greens_function_imaginary, grouped_per_block[1], precision=upper_bound)
        product_imaginary = jnp.einsum('kpn,pnj->pkj', greens_function_real, grouped_per_block[1], precision=upper_bound) + jnp.einsum('kpn,pnj->pkj', greens_function_imaginary, grouped_per_block[0], precision=upper_bound)
        test_real = grouped_per_block[0, block_a]
        test_imag = grouped_per_block[1, block_a]
        row_real = jnp.einsum('mk,bmc->kbc', test_real, product_real, precision=upper_bound) + jnp.einsum('mk,bmc->kbc', test_imag, product_imaginary, precision=upper_bound)
        row_imag = jnp.einsum('mk,bmc->kbc', test_real, product_imaginary, precision=upper_bound) - jnp.einsum('mk,bmc->kbc', test_imag, product_real, precision=upper_bound)
        return jnp.stack([row_real, row_imag]).reshape(2, NCBF, ORDER)
    rows = lax.map(one_row, jnp.arange(BLOCKS, dtype=jnp.int32))
    system_matrix = jnp.transpose(rows, (1, 0, 2, 3)).reshape(2, ORDER, ORDER)

    def slot_rows(full):
        return full.reshape(2, BLOCKS, NCBF, ORDER)[:, block_of_slot].reshape(2, ORDER, ORDER)
    reduced = slot_rows(system_matrix)
    for step in range(PANELS):
        start = (panel_order[step] * NCBF).astype(jnp.int32)
        upper = lax.dynamic_slice_in_dim(system_matrix, start, NCBF, 1)
        column = lax.dynamic_slice_in_dim(system_matrix, start, NCBF, 2)
        pivot = lax.dynamic_slice_in_dim(upper, start, NCBF, 2)
        sol_real, sol_imag = solve_pivot(pivot, upper)
        upd_real = jnp.dot(column[0], sol_real, precision=upper_bound) - jnp.dot(column[1], sol_imag, precision=upper_bound)
        upd_imag = jnp.dot(column[0], sol_imag, precision=upper_bound) + jnp.dot(column[1], sol_real, precision=upper_bound)
        system_matrix = system_matrix - jnp.stack([upd_real, upd_imag])
    return (reduced, slot_rows(system_matrix))
```

```python
import functools

import jax
import jax.numpy as jnp
from jax import lax
from jax.experimental import pallas as pl
from jax.experimental.pallas import tpu as pltpu
from jax.sharding import PartitionSpec as P

PANELS = 2

SELF_REAL = 12.0
SELF_IMAG = -3.0
COUPLE = 2.0
WAVE = 1.3

COS_TURN = (0.999999211770312, -19.738980419471126, 64.92865850463285, -85.27162830146948,
            58.79050662870376, -21.071108461771125)
SIN_TURN = (6.283184916984331, -41.34158926418157, 81.59994386455666, -76.61447586020026,
            41.342889428722025, -12.471244745942547)
TURNS = WAVE / (2.0 * 3.141592653589793)

HIGH = lax.Precision.HIGHEST


def horner(coefs, x):
    total = jnp.full_like(x, coefs[-1])
    for c in coefs[-2::-1]:
        total = total * x + c
    return total


def green_kernel(test_ref, basis_ref, out_ref):
    rows = out_ref.shape[1]
    unk = basis_ref.shape[2]
    chunk = 16

    def body(i, _):
        start = pl.multiple_of(i * chunk, chunk)
        test = test_ref[pl.ds(start, chunk), :]
        squared = None
        for which in range(3):
            spacing = test[:, which:which + 1] - basis_ref[0, which:which + 1, :]
            term = spacing * spacing
            squared = term if squared is None else squared + term
        coincide = squared == 0.0
        bounded = jnp.maximum(squared, 1.0)
        inverted = lax.rsqrt(bounded)
        turns = bounded * inverted * TURNS
        frac = turns - jnp.floor(turns + 0.5)
        frac2 = frac * frac
        scaled = COUPLE * inverted
        real = jnp.where(coincide, SELF_REAL, scaled * horner(COS_TURN, frac2))
        imag = jnp.where(coincide, SELF_IMAG, -(scaled * frac) * horner(SIN_TURN, frac2))
        out_ref[0, pl.ds(start, chunk), :unk] = real.astype(jnp.bfloat16)
        out_ref[0, pl.ds(start, chunk), unk:] = imag.astype(jnp.bfloat16)
        return 0

    lax.fori_loop(0, rows // chunk, body, 0)


def green_tiles(test_pos, basis_pos):
    unk = test_pos.shape[0]
    slab = basis_pos.shape[0]
    rows = min(256, unk)
    return pl.pallas_call(
        green_kernel,
        grid=(slab, unk // rows),
        in_specs=[
            pl.BlockSpec((rows, 3), lambda s, i: (i, 0)),
            pl.BlockSpec((1, 3, unk), lambda s, i: (s, 0, 0)),
        ],
        out_specs=pl.BlockSpec((1, rows, 2 * unk), lambda s, i: (s, i, 0)),
        out_shape=jax.ShapeDtypeStruct((slab, unk, 2 * unk), jnp.bfloat16),
        cost_estimate=pl.CostEstimate(
            flops=slab * unk * unk * 6000, bytes_accessed=slab * unk * unk * 4, transcendentals=slab * unk * unk
        ),
        name="green",
    )(test_pos, basis_pos)


def couple_kernel(green_ref, basis_ref, tested_ref, out_ref):
    real, imag = basis_ref[0, 0], basis_ref[1, 0]
    funcs = real.shape[1]
    top = jnp.concatenate([real, imag], axis=1)
    low = jnp.concatenate([-imag, real], axis=1)
    packed = jnp.concatenate([top, low], axis=0)
    product = jnp.dot(green_ref[0], packed, preferred_element_type=jnp.float32)
    high = product.astype(jnp.bfloat16)
    rest = (product - high.astype(jnp.float32)).astype(jnp.bfloat16)
    tested = tested_ref[...]
    outer = jnp.dot(tested, high, preferred_element_type=jnp.float32) + jnp.dot(
        tested, rest, preferred_element_type=jnp.float32
    )
    out_ref[0] = outer[:funcs, :funcs] + outer[funcs:, funcs:]
    out_ref[1] = outer[:funcs, funcs:] - outer[funcs:, :funcs]


def couple(green, slab_basis, tested):
    slab, unk, _ = green.shape
    funcs = slab_basis.shape[3]
    return pl.pallas_call(
        couple_kernel,
        grid=(slab,),
        in_specs=[
            pl.BlockSpec((1, unk, 2 * unk), lambda s: (s, 0, 0)),
            pl.BlockSpec((2, 1, unk, funcs), lambda s: (0, s, 0, 0)),
            pl.BlockSpec((2 * funcs, unk), lambda s: (0, 0)),
        ],
        out_specs=pl.BlockSpec((2, funcs, funcs), lambda s: (0, 0, s)),
        out_shape=jax.ShapeDtypeStruct((2, funcs, slab * funcs), jnp.float32),
        compiler_params=pltpu.CompilerParams(vmem_limit_bytes=40 * 1024 * 1024),
        cost_estimate=pl.CostEstimate(
            flops=slab * unk * unk * funcs * 8, bytes_accessed=slab * unk * unk * 4, transcendentals=0
        ),
        name="couple",
    )(green, slab_basis, tested)


def cdot(a, b):
    m, n = a[0].shape[0], b[0].shape[1]
    left = jnp.concatenate(a, axis=0)
    right = jnp.concatenate(b, axis=1)
    outer = jnp.dot(left, right, precision=HIGH, preferred_element_type=jnp.float32)
    return (outer[:m, :n] - outer[m:, n:], outer[:m, n:] + outer[m:, :n])


def csub(a, b):
    return (a[0] - b[0], a[1] - b[1])


def cadd(a, b):
    return (a[0] + b[0], a[1] + b[1])


def hermitian_inverse(herm):
    n = herm[0].shape[0]
    group = 8
    lane = lax.broadcasted_iota(jnp.int32, (1, n), 1)
    sub = lax.broadcasted_iota(jnp.int32, (group, 1), 0)

    def turn(_, carried):
        real, imag = carried
        head_r, head_i = real[:group], imag[:group]
        tail_r, tail_i = real[group:], imag[group:]
        for j in range(group):
            here = lane == j
            mine = sub == j
            row_r, row_i = head_r[j:j + 1, :], head_i[j:j + 1, :]
            scale = 1.0 / row_r[:, j:j + 1]
            row_r = jnp.where(here, 1.0, row_r) * scale
            row_i = jnp.where(here, 0.0, row_i) * scale
            col_r, col_i = tail_r[:, j:j + 1], tail_i[:, j:j + 1]
            tail_r = jnp.where(here, 0.0, tail_r) - col_r * row_r + col_i * row_i
            tail_i = jnp.where(here, 0.0, tail_i) - col_r * row_i - col_i * row_r
            col_r = jnp.where(mine, -1.0, head_r[:, j:j + 1])
            col_i = jnp.where(mine, 0.0, head_i[:, j:j + 1])
            gone = here | mine
            head_r = jnp.where(gone, 0.0, head_r) - col_r * row_r + col_i * row_i
            head_i = jnp.where(gone, 0.0, head_i) - col_r * row_i - col_i * row_r
        real = pltpu.roll(jnp.concatenate([tail_r, head_r], axis=0), n - group, 1)
        imag = pltpu.roll(jnp.concatenate([tail_i, head_i], axis=0), n - group, 1)
        return real, imag

    return lax.fori_loop(0, n // group, turn, herm)


def inverse_of(d):
    n = d[0].shape[0]
    adjoint = (d[0].T, -d[1].T)
    guess = cdot(hermitian_inverse(cdot(adjoint, d)), adjoint)
    off = cdot(d, guess)
    row = lax.broadcasted_iota(jnp.int32, (n, n), 0)
    col = lax.broadcasted_iota(jnp.int32, (n, n), 1)
    unit = jnp.where(row == col, 1.0, 0.0)
    return cadd(guess, cdot(guess, (unit - off[0], -off[1])))


def pivot_kernel(d_ref, first_ref, joint_ref, second_ref):
    def tile(i, j):
        return (d_ref[i, j, 0], d_ref[i, j, 1])

    first = inverse_of(tile(0, 0))
    joint = cdot(first, tile(0, 1))
    second = inverse_of(csub(tile(1, 1), cdot(tile(1, 0), joint)))
    for ref, value in ((first_ref, first), (joint_ref, joint), (second_ref, second)):
        ref[0] = value[0]
        ref[1] = value[1]


def pivot_inverses(pivots):
    funcs = pivots.shape[3]
    shape = jax.ShapeDtypeStruct((2, funcs, funcs), jnp.float32)
    return pl.pallas_call(
        pivot_kernel,
        out_shape=(shape, shape, shape),
        compiler_params=pltpu.CompilerParams(vmem_limit_bytes=32 * 1024 * 1024),
        cost_estimate=pl.CostEstimate(flops=20_000_000_000, bytes_accessed=1_000_000, transcendentals=0),
        name="pivots",
    )(pivots)


def update_kernel(full_ref, rows_ref, cols_ref, low_ref, first_ref, joint_ref, second_ref, out_ref):
    def pair(ref):
        return (ref[0], ref[1])

    upper0 = (rows_ref[0, 0], rows_ref[0, 1])
    upper1 = (rows_ref[1, 0], rows_ref[1, 1])
    begun = cdot(pair(first_ref), upper0)
    sol1 = cdot(pair(second_ref), csub(upper1, cdot(pair(low_ref), begun)))
    sol0 = csub(begun, cdot(pair(joint_ref), sol1))
    taken = cadd(
        cdot((cols_ref[0, 0], cols_ref[0, 1]), sol0), cdot((cols_ref[1, 0], cols_ref[1, 1]), sol1)
    )
    out_ref[0] = full_ref[0] - taken[0]
    out_ref[1] = full_ref[1] - taken[1]


def update(full, rows, cols, low, first, joint, second):
    return pl.pallas_call(
        update_kernel,
        out_shape=jax.ShapeDtypeStruct(full.shape, jnp.float32),
        compiler_params=pltpu.CompilerParams(vmem_limit_bytes=32 * 1024 * 1024),
        cost_estimate=pl.CostEstimate(flops=2_000_000_000, bytes_accessed=2_000_000, transcendentals=0),
        name="update",
    )(full, rows, cols, low, first, joint, second)


def on_device(inverse, excite, coordinates, block_of_slot, panel_order):
    funcs = excite.shape[3]
    blocks = block_of_slot.shape[0]
    grp_index = lax.axis_index("grp")
    slab_count = blocks // lax.axis_size("grp")
    own_id = block_of_slot[lax.axis_index("blk")]

    exc_r, exc_i = excite[0, 0], excite[1, 0]
    right_r = jnp.concatenate([exc_r, exc_i], axis=1)
    right_i = jnp.concatenate([-exc_i, exc_r], axis=1)
    rows = jnp.dot(inverse[0, 0], right_r, preferred_element_type=jnp.float32) + jnp.dot(
        inverse[1, 0], right_i, preferred_element_type=jnp.float32
    )
    basis_rows = jnp.stack([rows[:, :funcs], rows[:, funcs:]]).astype(jnp.bfloat16)[:, None]

    places = coordinates.astype(jnp.float32)
    own_pos = lax.dynamic_index_in_dim(places, own_id, 1, keepdims=False).T
    slab_pos = lax.dynamic_slice_in_dim(places, grp_index * slab_count, slab_count, 1)
    green = green_tiles(own_pos, jnp.transpose(slab_pos, (1, 0, 2)))

    sliced = lax.all_gather(basis_rows, "blk", axis=1, tiled=True)
    slots = jnp.arange(blocks, dtype=jnp.int32)
    grouped = jnp.concatenate(
        [
            lax.dynamic_slice_in_dim(sliced, jnp.sum(jnp.where(block_of_slot == b, slots, 0)), 1, 1)
            for b in range(blocks)
        ],
        axis=1,
    )
    slab = lax.all_to_all(grouped, "grp", split_axis=1, concat_axis=2, tiled=True)
    own_full = lax.all_gather(basis_rows, "grp", axis=2, tiled=True)[:, 0]
    tested = jnp.transpose(own_full, (0, 2, 1)).reshape(2 * funcs, -1)

    reduced = couple(green, slab, tested)

    row_mine = [own_id == panel_order[q] for q in range(PANELS)]
    col_mine = [panel_order[q] // slab_count == grp_index for q in range(PANELS)]
    cols = jnp.stack([
        jnp.where(
            col_mine[q],
            lax.dynamic_slice_in_dim(reduced, (panel_order[q] % slab_count) * funcs, funcs, 2),
            0.0,
        )
        for q in range(PANELS)
    ])
    pivots = jnp.stack([jnp.where(row_mine[q], cols, 0.0) for q in range(PANELS)])
    pivots = lax.psum(pivots, ("blk", "grp"))
    upper = lax.psum(jnp.stack([jnp.where(row_mine[q], reduced, 0.0) for q in range(PANELS)]), "blk")
    cols = lax.psum(cols, "grp")
    first, joint, second = pivot_inverses(pivots)
    schur = update(reduced, upper, cols, pivots[1, 0], first, joint, second)
    return (reduced, schur)


def solution(mesh):
    placed = (P(None, "blk", "grp", None), P(None, "blk", None, None), P(), P(), P())
    return jax.shard_map(
        on_device,
        mesh=mesh,
        in_specs=placed,
        out_specs=(P(None, "blk", "grp"), P(None, "blk", "grp")),
        check_vma=False,
    )
```

```python
import functools

import jax
import jax.numpy as jnp
from jax import lax
from jax.experimental import pallas as pl
from jax.experimental.pallas import tpu as pltpu
from jax.sharding import PartitionSpec as P

PANELS = 2

SELF_REAL = 12.0
SELF_IMAG = -3.0
COUPLE = 2.0
WAVE = 1.3

COS_TURN = (0.999999211770312, -19.738980419471126, 64.92865850463285, -85.27162830146948,
            58.79050662870376, -21.071108461771125)
SIN_TURN = (6.283184916984331, -41.34158926418157, 81.59994386455666, -76.61447586020026,
            41.342889428722025, -12.471244745942547)
TURNS = WAVE / (2.0 * 3.141592653589793)

HIGH = lax.Precision.HIGHEST


def horner(coefs, x):
    total = jnp.full_like(x, coefs[-1])
    for c in coefs[-2::-1]:
        total = total * x + c
    return total


def gather_kernel(axis, peers, count, *refs):
    sources, targets = refs[:count], refs[count:2 * count]
    send_sem, recv_sem, local_sem = refs[2 * count:]
    me = lax.axis_index(axis)
    barrier = pltpu.get_barrier_semaphore()
    for step in range(1, peers):
        pl.semaphore_signal(
            barrier, inc=1, device_id={axis: lax.rem(me + step, peers)}, device_id_type=pl.DeviceIdType.MESH
        )
    pl.semaphore_wait(barrier, peers - 1)

    def sent(which, step):
        return pltpu.make_async_remote_copy(
            src_ref=sources[which],
            dst_ref=targets[which].at[me],
            send_sem=send_sem.at[which, step - 1],
            recv_sem=recv_sem.at[which, step - 1],
            device_id={axis: lax.rem(me + step, peers)},
            device_id_type=pl.DeviceIdType.MESH,
        )

    copies = [sent(which, step) for step in range(1, peers) for which in range(count)]
    kept = [
        pltpu.make_async_copy(sources[which], targets[which].at[me], local_sem.at[which])
        for which in range(count)
    ]
    for copy in copies + kept:
        copy.start()
    for copy in kept + copies:
        copy.wait()


def gather(axis, collective_id, *values):
    peers = lax.axis_size(axis)
    count = len(values)
    anywhere = pl.BlockSpec(memory_space=pl.ANY)
    return pl.pallas_call(
        functools.partial(gather_kernel, axis, peers, count),
        in_specs=[anywhere] * count,
        out_specs=[anywhere] * count,
        out_shape=[jax.ShapeDtypeStruct((peers,) + v.shape, v.dtype) for v in values],
        scratch_shapes=[
            pltpu.SemaphoreType.DMA((count, peers - 1)),
            pltpu.SemaphoreType.DMA((count, peers - 1)),
            pltpu.SemaphoreType.DMA((count,)),
        ],
        compiler_params=pltpu.CompilerParams(collective_id=collective_id, has_side_effects=True),
        name="gather_" + axis + str(collective_id),
    )(*values)


def green_kernel(test_ref, basis_ref, out_ref):
    rows = out_ref.shape[1]
    unk = basis_ref.shape[2]
    chunk = 16

    def body(i, _):
        start = pl.multiple_of(i * chunk, chunk)
        test = test_ref[pl.ds(start, chunk), :]
        squared = None
        for which in range(3):
            spacing = test[:, which:which + 1] - basis_ref[0, which:which + 1, :]
            term = spacing * spacing
            squared = term if squared is None else squared + term
        coincide = squared == 0.0
        bounded = jnp.maximum(squared, 1.0)
        inverted = lax.rsqrt(bounded)
        turns = bounded * inverted * TURNS
        frac = turns - jnp.floor(turns + 0.5)
        frac2 = frac * frac
        scaled = COUPLE * inverted
        real = jnp.where(coincide, SELF_REAL, scaled * horner(COS_TURN, frac2))
        imag = jnp.where(coincide, SELF_IMAG, -(scaled * frac) * horner(SIN_TURN, frac2))
        out_ref[0, pl.ds(start, chunk), :unk] = real.astype(jnp.bfloat16)
        out_ref[0, pl.ds(start, chunk), unk:] = imag.astype(jnp.bfloat16)
        return 0

    lax.fori_loop(0, rows // chunk, body, 0)


def green_tiles(test_pos, basis_pos):
    unk = test_pos.shape[0]
    slab = basis_pos.shape[0]
    rows = min(256, unk)
    return pl.pallas_call(
        green_kernel,
        grid=(slab, unk // rows),
        in_specs=[
            pl.BlockSpec((rows, 3), lambda s, i: (i, 0)),
            pl.BlockSpec((1, 3, unk), lambda s, i: (s, 0, 0)),
        ],
        out_specs=pl.BlockSpec((1, rows, 2 * unk), lambda s, i: (s, i, 0)),
        out_shape=jax.ShapeDtypeStruct((slab, unk, 2 * unk), jnp.bfloat16),
        cost_estimate=pl.CostEstimate(
            flops=slab * unk * unk * 6000, bytes_accessed=slab * unk * unk * 4, transcendentals=slab * unk * unk
        ),
        name="green",
    )(test_pos, basis_pos)


def couple_kernel(green_ref, basis_ref, tested_ref, out_ref):
    real, imag = basis_ref[0, 0], basis_ref[1, 0]
    funcs = real.shape[1]
    top = jnp.concatenate([real, imag], axis=1)
    low = jnp.concatenate([-imag, real], axis=1)
    packed = jnp.concatenate([top, low], axis=0)
    product = jnp.dot(green_ref[0], packed, preferred_element_type=jnp.float32)
    high = product.astype(jnp.bfloat16)
    rest = (product - high.astype(jnp.float32)).astype(jnp.bfloat16)
    tested = tested_ref[...]
    outer = jnp.dot(tested, high, preferred_element_type=jnp.float32) + jnp.dot(
        tested, rest, preferred_element_type=jnp.float32
    )
    out_ref[0] = outer[:funcs, :funcs] + outer[funcs:, funcs:]
    out_ref[1] = outer[:funcs, funcs:] - outer[funcs:, :funcs]


def couple(green, slab_basis, tested):
    slab, unk, _ = green.shape
    funcs = slab_basis.shape[3]
    return pl.pallas_call(
        couple_kernel,
        grid=(slab,),
        in_specs=[
            pl.BlockSpec((1, unk, 2 * unk), lambda s: (s, 0, 0)),
            pl.BlockSpec((2, 1, unk, funcs), lambda s: (0, s, 0, 0)),
            pl.BlockSpec((2 * funcs, unk), lambda s: (0, 0)),
        ],
        out_specs=pl.BlockSpec((2, funcs, funcs), lambda s: (0, 0, s)),
        out_shape=jax.ShapeDtypeStruct((2, funcs, slab * funcs), jnp.float32),
        compiler_params=pltpu.CompilerParams(vmem_limit_bytes=40 * 1024 * 1024),
        cost_estimate=pl.CostEstimate(
            flops=slab * unk * unk * funcs * 8, bytes_accessed=slab * unk * unk * 4, transcendentals=0
        ),
        name="couple",
    )(green, slab_basis, tested)


def cdot(a, b):
    m, n = a[0].shape[0], b[0].shape[1]
    left = jnp.concatenate(a, axis=0)
    right = jnp.concatenate(b, axis=1)
    outer = jnp.dot(left, right, precision=HIGH, preferred_element_type=jnp.float32)
    return (outer[:m, :n] - outer[m:, n:], outer[:m, n:] + outer[m:, :n])


def csub(a, b):
    return (a[0] - b[0], a[1] - b[1])


def cadd(a, b):
    return (a[0] + b[0], a[1] + b[1])


def hermitian_inverse(herm):
    n = herm[0].shape[0]
    group = 8
    lane = lax.broadcasted_iota(jnp.int32, (1, n), 1)
    sub = lax.broadcasted_iota(jnp.int32, (group, 1), 0)

    def turn(_, carried):
        real, imag = carried
        head_r, head_i = real[:group], imag[:group]
        tail_r, tail_i = real[group:], imag[group:]
        for j in range(group):
            here = lane == j
            mine = sub == j
            row_r, row_i = head_r[j:j + 1, :], head_i[j:j + 1, :]
            scale = 1.0 / row_r[:, j:j + 1]
            row_r = jnp.where(here, 1.0, row_r) * scale
            row_i = jnp.where(here, 0.0, row_i) * scale
            col_r, col_i = tail_r[:, j:j + 1], tail_i[:, j:j + 1]
            tail_r = jnp.where(here, 0.0, tail_r) - col_r * row_r + col_i * row_i
            tail_i = jnp.where(here, 0.0, tail_i) - col_r * row_i - col_i * row_r
            col_r = jnp.where(mine, -1.0, head_r[:, j:j + 1])
            col_i = jnp.where(mine, 0.0, head_i[:, j:j + 1])
            gone = here | mine
            head_r = jnp.where(gone, 0.0, head_r) - col_r * row_r + col_i * row_i
            head_i = jnp.where(gone, 0.0, head_i) - col_r * row_i - col_i * row_r
        real = pltpu.roll(jnp.concatenate([tail_r, head_r], axis=0), n - group, 1)
        imag = pltpu.roll(jnp.concatenate([tail_i, head_i], axis=0), n - group, 1)
        return real, imag

    return lax.fori_loop(0, n // group, turn, herm)


def inverse_of(d):
    n = d[0].shape[0]
    adjoint = (d[0].T, -d[1].T)
    guess = cdot(hermitian_inverse(cdot(adjoint, d)), adjoint)
    off = cdot(d, guess)
    row = lax.broadcasted_iota(jnp.int32, (n, n), 0)
    col = lax.broadcasted_iota(jnp.int32, (n, n), 1)
    unit = jnp.where(row == col, 1.0, 0.0)
    return cadd(guess, cdot(guess, (unit - off[0], -off[1])))


def pivot_kernel(d_ref, first_ref, joint_ref, second_ref):
    def tile(i, j):
        return (d_ref[i, j, 0], d_ref[i, j, 1])

    first = inverse_of(tile(0, 0))
    joint = cdot(first, tile(0, 1))
    second = inverse_of(csub(tile(1, 1), cdot(tile(1, 0), joint)))
    for ref, value in ((first_ref, first), (joint_ref, joint), (second_ref, second)):
        ref[0] = value[0]
        ref[1] = value[1]


def pivot_inverses(pivots):
    funcs = pivots.shape[3]
    shape = jax.ShapeDtypeStruct((2, funcs, funcs), jnp.float32)
    return pl.pallas_call(
        pivot_kernel,
        out_shape=(shape, shape, shape),
        compiler_params=pltpu.CompilerParams(vmem_limit_bytes=32 * 1024 * 1024),
        cost_estimate=pl.CostEstimate(flops=20_000_000_000, bytes_accessed=1_000_000, transcendentals=0),
        name="pivots",
    )(pivots)


def update_kernel(full_ref, rows_ref, cols_ref, low_ref, first_ref, joint_ref, second_ref, out_ref):
    def pair(ref):
        return (ref[0], ref[1])

    upper0 = (rows_ref[0, 0], rows_ref[0, 1])
    upper1 = (rows_ref[1, 0], rows_ref[1, 1])
    begun = cdot(pair(first_ref), upper0)
    sol1 = cdot(pair(second_ref), csub(upper1, cdot(pair(low_ref), begun)))
    sol0 = csub(begun, cdot(pair(joint_ref), sol1))
    taken = cadd(
        cdot((cols_ref[0, 0], cols_ref[0, 1]), sol0), cdot((cols_ref[1, 0], cols_ref[1, 1]), sol1)
    )
    out_ref[0] = full_ref[0] - taken[0]
    out_ref[1] = full_ref[1] - taken[1]


def update(full, rows, cols, low, first, joint, second):
    return pl.pallas_call(
        update_kernel,
        out_shape=jax.ShapeDtypeStruct(full.shape, jnp.float32),
        compiler_params=pltpu.CompilerParams(vmem_limit_bytes=32 * 1024 * 1024),
        cost_estimate=pl.CostEstimate(flops=2_000_000_000, bytes_accessed=2_000_000, transcendentals=0),
        name="update",
    )(full, rows, cols, low, first, joint, second)


def on_device(inverse, excite, coordinates, block_of_slot, panel_order):
    funcs = excite.shape[3]
    blocks = block_of_slot.shape[0]
    grp_index = lax.axis_index("grp")
    slab_count = blocks // lax.axis_size("grp")
    own_id = block_of_slot[lax.axis_index("blk")]

    exc_r, exc_i = excite[0, 0], excite[1, 0]
    right_r = jnp.concatenate([exc_r, exc_i], axis=1)
    right_i = jnp.concatenate([-exc_i, exc_r], axis=1)
    rows = jnp.dot(inverse[0, 0], right_r, preferred_element_type=jnp.float32) + jnp.dot(
        inverse[1, 0], right_i, preferred_element_type=jnp.float32
    )
    basis_rows = jnp.stack([rows[:, :funcs], rows[:, funcs:]]).astype(jnp.bfloat16)

    places = coordinates.astype(jnp.float32)
    own_pos = lax.dynamic_index_in_dim(places, own_id, 1, keepdims=False).T
    slab_pos = lax.dynamic_slice_in_dim(places, grp_index * slab_count, slab_count, 1)
    green = green_tiles(own_pos, jnp.transpose(slab_pos, (1, 0, 2)))

    (sliced,) = gather("blk", 0, basis_rows)
    (whole,) = gather("grp", 1, basis_rows)
    slots = jnp.arange(blocks, dtype=jnp.int32)

    def slot_of(block):
        return jnp.sum(jnp.where(block_of_slot == block, slots, 0))

    grouped = jnp.concatenate(
        [lax.dynamic_index_in_dim(sliced, slot_of(b), 0, keepdims=True) for b in range(blocks)], axis=0
    )
    slab = lax.all_to_all(grouped, "grp", split_axis=0, concat_axis=2, tiled=True)
    slab = jnp.transpose(slab, (1, 0, 2, 3))
    tested = jnp.transpose(whole, (1, 3, 0, 2)).reshape(2 * funcs, -1)

    reduced = couple(green, slab, tested)

    tiles = jnp.stack([
        lax.dynamic_slice_in_dim(reduced, (panel_order[q] % slab_count) * funcs, funcs, 2)
        for q in range(PANELS)
    ])
    (spread,) = gather("grp", 2, tiles)
    cols = jnp.stack([
        lax.dynamic_index_in_dim(spread, panel_order[q] // slab_count, 0, keepdims=False)[q]
        for q in range(PANELS)
    ])
    all_rows, all_cols = gather("blk", 3, reduced, cols)
    places_of = [slot_of(panel_order[q]) for q in range(PANELS)]
    upper = jnp.stack([lax.dynamic_index_in_dim(all_rows, p, 0, keepdims=False) for p in places_of])
    pivots = jnp.stack([lax.dynamic_index_in_dim(all_cols, p, 0, keepdims=False) for p in places_of])
    first, joint, second = pivot_inverses(pivots)
    schur = update(reduced, upper, cols, pivots[1, 0], first, joint, second)
    return (reduced, schur)


def solution(mesh):
    placed = (P(None, "blk", "grp", None), P(None, "blk", None, None), P(), P(), P())
    return jax.shard_map(
        on_device,
        mesh=mesh,
        in_specs=placed,
        out_specs=(P(None, "blk", "grp"), P(None, "blk", "grp")),
        check_vma=False,
    )
```

```python
import functools

import jax
import jax.numpy as jnp
from jax import lax
from jax.experimental import pallas as pl
from jax.experimental.pallas import tpu as pltpu
from jax.sharding import PartitionSpec as P

PANELS = 2

SELF_REAL = 12.0
SELF_IMAG = -3.0
COUPLE = 2.0
WAVE = 1.3

COS_TURN = (0.999999211770312, -19.738980419471126, 64.92865850463285, -85.27162830146948,
            58.79050662870376, -21.071108461771125)
SIN_TURN = (6.283184916984331, -41.34158926418157, 81.59994386455666, -76.61447586020026,
            41.342889428722025, -12.471244745942547)
TURNS = WAVE / (2.0 * 3.141592653589793)

HIGH = lax.Precision.HIGHEST


def horner(coefs, x):
    total = jnp.full_like(x, coefs[-1])
    for c in coefs[-2::-1]:
        total = total * x + c
    return total


def gather_kernel(axis, peers, count, *refs):
    sources, targets = refs[:count], refs[count:2 * count]
    send_sem, recv_sem, local_sem = refs[2 * count:]
    me = lax.axis_index(axis)
    barrier = pltpu.get_barrier_semaphore()
    for step in range(1, peers):
        pl.semaphore_signal(
            barrier, inc=1, device_id={axis: lax.rem(me + step, peers)}, device_id_type=pl.DeviceIdType.MESH
        )
    pl.semaphore_wait(barrier, peers - 1)

    def sent(which, step):
        return pltpu.make_async_remote_copy(
            src_ref=sources[which],
            dst_ref=targets[which].at[me],
            send_sem=send_sem.at[which, step - 1],
            recv_sem=recv_sem.at[which, step - 1],
            device_id={axis: lax.rem(me + step, peers)},
            device_id_type=pl.DeviceIdType.MESH,
        )

    copies = [sent(which, step) for step in range(1, peers) for which in range(count)]
    kept = [
        pltpu.make_async_copy(sources[which], targets[which].at[me], local_sem.at[which])
        for which in range(count)
    ]
    for copy in copies + kept:
        copy.start()
    for copy in kept + copies:
        copy.wait()


def gather(axis, collective_id, *values):
    peers = lax.axis_size(axis)
    count = len(values)
    anywhere = pl.BlockSpec(memory_space=pl.ANY)
    return pl.pallas_call(
        functools.partial(gather_kernel, axis, peers, count),
        in_specs=[anywhere] * count,
        out_specs=[anywhere] * count,
        out_shape=[jax.ShapeDtypeStruct((peers,) + v.shape, v.dtype) for v in values],
        scratch_shapes=[
            pltpu.SemaphoreType.DMA((count, peers - 1)),
            pltpu.SemaphoreType.DMA((count, peers - 1)),
            pltpu.SemaphoreType.DMA((count,)),
        ],
        compiler_params=pltpu.CompilerParams(collective_id=collective_id, has_side_effects=True),
        name="gather_" + axis + str(collective_id),
    )(*values)


def green_kernel(test_ref, basis_ref, out_ref):
    rows = out_ref.shape[1]
    unk = basis_ref.shape[2]
    chunk = 16

    def body(i, _):
        start = pl.multiple_of(i * chunk, chunk)
        test = test_ref[pl.ds(start, chunk), :]
        squared = None
        for which in range(3):
            spacing = test[:, which:which + 1] - basis_ref[0, which:which + 1, :]
            term = spacing * spacing
            squared = term if squared is None else squared + term
        coincide = squared == 0.0
        bounded = jnp.maximum(squared, 1.0)
        inverted = lax.rsqrt(bounded)
        turns = bounded * inverted * TURNS
        frac = turns - jnp.floor(turns + 0.5)
        frac2 = frac * frac
        scaled = COUPLE * inverted
        real = jnp.where(coincide, SELF_REAL, scaled * horner(COS_TURN, frac2))
        imag = jnp.where(coincide, SELF_IMAG, -(scaled * frac) * horner(SIN_TURN, frac2))
        out_ref[0, pl.ds(start, chunk), :unk] = real.astype(jnp.bfloat16)
        out_ref[0, pl.ds(start, chunk), unk:] = imag.astype(jnp.bfloat16)
        return 0

    lax.fori_loop(0, rows // chunk, body, 0)


def green_tiles(test_pos, basis_pos):
    unk = test_pos.shape[0]
    slab = basis_pos.shape[0]
    rows = min(256, unk)
    return pl.pallas_call(
        green_kernel,
        grid=(slab, unk // rows),
        in_specs=[
            pl.BlockSpec((rows, 3), lambda s, i: (i, 0)),
            pl.BlockSpec((1, 3, unk), lambda s, i: (s, 0, 0)),
        ],
        out_specs=pl.BlockSpec((1, rows, 2 * unk), lambda s, i: (s, i, 0)),
        out_shape=jax.ShapeDtypeStruct((slab, unk, 2 * unk), jnp.bfloat16),
        cost_estimate=pl.CostEstimate(
            flops=slab * unk * unk * 6000, bytes_accessed=slab * unk * unk * 4, transcendentals=slab * unk * unk
        ),
        name="green",
    )(test_pos, basis_pos)


def couple_kernel(green_ref, basis_ref, tested_ref, out_ref):
    real, imag = basis_ref[0, 0], basis_ref[1, 0]
    funcs = real.shape[1]
    top = jnp.concatenate([real, imag], axis=1)
    low = jnp.concatenate([-imag, real], axis=1)
    packed = jnp.concatenate([top, low], axis=0)
    product = jnp.dot(green_ref[0], packed, preferred_element_type=jnp.float32)
    high = product.astype(jnp.bfloat16)
    rest = (product - high.astype(jnp.float32)).astype(jnp.bfloat16)
    tested = tested_ref[...]
    outer = jnp.dot(tested, high, preferred_element_type=jnp.float32) + jnp.dot(
        tested, rest, preferred_element_type=jnp.float32
    )
    out_ref[0] = outer[:funcs, :funcs] + outer[funcs:, funcs:]
    out_ref[1] = outer[:funcs, funcs:] - outer[funcs:, :funcs]


def couple(green, slab_basis, tested):
    slab, unk, _ = green.shape
    funcs = slab_basis.shape[3]
    return pl.pallas_call(
        couple_kernel,
        grid=(slab,),
        in_specs=[
            pl.BlockSpec((1, unk, 2 * unk), lambda s: (s, 0, 0)),
            pl.BlockSpec((2, 1, unk, funcs), lambda s: (0, s, 0, 0)),
            pl.BlockSpec((2 * funcs, unk), lambda s: (0, 0)),
        ],
        out_specs=pl.BlockSpec((2, funcs, funcs), lambda s: (0, 0, s)),
        out_shape=jax.ShapeDtypeStruct((2, funcs, slab * funcs), jnp.float32),
        compiler_params=pltpu.CompilerParams(vmem_limit_bytes=40 * 1024 * 1024),
        cost_estimate=pl.CostEstimate(
            flops=slab * unk * unk * funcs * 8, bytes_accessed=slab * unk * unk * 4, transcendentals=0
        ),
        name="couple",
    )(green, slab_basis, tested)


def cdot(a, b):
    m, n = a[0].shape[0], b[0].shape[1]
    left = jnp.concatenate(a, axis=0)
    right = jnp.concatenate(b, axis=1)
    outer = jnp.dot(left, right, precision=HIGH, preferred_element_type=jnp.float32)
    return (outer[:m, :n] - outer[m:, n:], outer[:m, n:] + outer[m:, :n])


def csub(a, b):
    return (a[0] - b[0], a[1] - b[1])


def cadd(a, b):
    return (a[0] + b[0], a[1] + b[1])


def hermitian_inverse(herm):
    n = herm[0].shape[0]
    group = 8
    lane = lax.broadcasted_iota(jnp.int32, (1, n), 1)
    sub = lax.broadcasted_iota(jnp.int32, (group, 1), 0)

    def turn(_, carried):
        real, imag = carried
        head_r, head_i = real[:group], imag[:group]
        tail_r, tail_i = real[group:], imag[group:]
        for j in range(group):
            here = lane == j
            mine = sub == j
            row_r, row_i = head_r[j:j + 1, :], head_i[j:j + 1, :]
            scale = 1.0 / row_r[:, j:j + 1]
            row_r = jnp.where(here, 1.0, row_r) * scale
            row_i = jnp.where(here, 0.0, row_i) * scale
            col_r, col_i = tail_r[:, j:j + 1], tail_i[:, j:j + 1]
            tail_r = jnp.where(here, 0.0, tail_r) - col_r * row_r + col_i * row_i
            tail_i = jnp.where(here, 0.0, tail_i) - col_r * row_i - col_i * row_r
            col_r = jnp.where(mine, -1.0, head_r[:, j:j + 1])
            col_i = jnp.where(mine, 0.0, head_i[:, j:j + 1])
            gone = here | mine
            head_r = jnp.where(gone, 0.0, head_r) - col_r * row_r + col_i * row_i
            head_i = jnp.where(gone, 0.0, head_i) - col_r * row_i - col_i * row_r
        real = pltpu.roll(jnp.concatenate([tail_r, head_r], axis=0), n - group, 1)
        imag = pltpu.roll(jnp.concatenate([tail_i, head_i], axis=0), n - group, 1)
        return real, imag

    return lax.fori_loop(0, n // group, turn, herm)


def inverse_of(d):
    n = d[0].shape[0]
    adjoint = (d[0].T, -d[1].T)
    guess = cdot(hermitian_inverse(cdot(adjoint, d)), adjoint)
    off = cdot(d, guess)
    row = lax.broadcasted_iota(jnp.int32, (n, n), 0)
    col = lax.broadcasted_iota(jnp.int32, (n, n), 1)
    unit = jnp.where(row == col, 1.0, 0.0)
    return cadd(guess, cdot(guess, (unit - off[0], -off[1])))


def pivot_kernel(d_ref, first_ref, joint_ref, second_ref):
    def tile(i, j):
        return (d_ref[i, j, 0], d_ref[i, j, 1])

    first = inverse_of(tile(0, 0))
    joint = cdot(first, tile(0, 1))
    second = inverse_of(csub(tile(1, 1), cdot(tile(1, 0), joint)))
    for ref, value in ((first_ref, first), (joint_ref, joint), (second_ref, second)):
        ref[0] = value[0]
        ref[1] = value[1]


def pivot_inverses(pivots):
    funcs = pivots.shape[3]
    shape = jax.ShapeDtypeStruct((2, funcs, funcs), jnp.float32)
    return pl.pallas_call(
        pivot_kernel,
        out_shape=(shape, shape, shape),
        compiler_params=pltpu.CompilerParams(vmem_limit_bytes=32 * 1024 * 1024),
        cost_estimate=pl.CostEstimate(flops=20_000_000_000, bytes_accessed=1_000_000, transcendentals=0),
        name="pivots",
    )(pivots)


def update_kernel(full_ref, rows_ref, cols_ref, low_ref, first_ref, joint_ref, second_ref, out_ref):
    def pair(ref):
        return (ref[0], ref[1])

    upper0 = (rows_ref[0, 0], rows_ref[0, 1])
    upper1 = (rows_ref[1, 0], rows_ref[1, 1])
    begun = cdot(pair(first_ref), upper0)
    sol1 = cdot(pair(second_ref), csub(upper1, cdot(pair(low_ref), begun)))
    sol0 = csub(begun, cdot(pair(joint_ref), sol1))
    taken = cadd(
        cdot((cols_ref[0, 0], cols_ref[0, 1]), sol0), cdot((cols_ref[1, 0], cols_ref[1, 1]), sol1)
    )
    out_ref[0] = full_ref[0] - taken[0]
    out_ref[1] = full_ref[1] - taken[1]


def update(full, rows, cols, low, first, joint, second):
    return pl.pallas_call(
        update_kernel,
        out_shape=jax.ShapeDtypeStruct(full.shape, jnp.float32),
        compiler_params=pltpu.CompilerParams(vmem_limit_bytes=32 * 1024 * 1024),
        cost_estimate=pl.CostEstimate(flops=2_000_000_000, bytes_accessed=2_000_000, transcendentals=0),
        name="update",
    )(full, rows, cols, low, first, joint, second)


def on_device(inverse, excite, coordinates, block_of_slot, panel_order):
    funcs = excite.shape[3]
    blocks = block_of_slot.shape[0]
    grp_index = lax.axis_index("grp")
    slab_count = blocks // lax.axis_size("grp")
    own_id = block_of_slot[lax.axis_index("blk")]

    exc_r, exc_i = excite[0, 0], excite[1, 0]
    right_r = jnp.concatenate([exc_r, exc_i], axis=1)
    right_i = jnp.concatenate([-exc_i, exc_r], axis=1)
    rows = jnp.dot(inverse[0, 0], right_r, preferred_element_type=jnp.float32) + jnp.dot(
        inverse[1, 0], right_i, preferred_element_type=jnp.float32
    )
    basis_rows = jnp.stack([rows[:, :funcs], rows[:, funcs:]]).astype(jnp.bfloat16)

    places = coordinates.astype(jnp.float32)
    own_pos = lax.dynamic_index_in_dim(places, own_id, 1, keepdims=False).T
    slab_pos = lax.dynamic_slice_in_dim(places, grp_index * slab_count, slab_count, 1)
    green = green_tiles(own_pos, jnp.transpose(slab_pos, (1, 0, 2)))

    (whole,) = gather("grp", 1, basis_rows)
    whole, basis_rows = lax.optimization_barrier((whole, basis_rows))
    (sliced,) = gather("blk", 0, basis_rows)
    slots = jnp.arange(blocks, dtype=jnp.int32)

    def slot_of(block):
        return jnp.sum(jnp.where(block_of_slot == block, slots, 0))

    chosen = (block_of_slot[None, :] == slots[:, None])[:, :, None, None, None]
    grouped = jnp.sum(jnp.where(chosen, sliced[None], 0), axis=1, dtype=jnp.float32).astype(jnp.bfloat16)
    slab = lax.all_to_all(grouped, "grp", split_axis=0, concat_axis=2, tiled=True)
    slab = jnp.transpose(slab, (1, 0, 2, 3))
    tested = jnp.transpose(whole, (1, 3, 0, 2)).reshape(2 * funcs, -1)

    reduced = couple(green, slab, tested)

    tiles = jnp.stack([
        lax.dynamic_slice_in_dim(reduced, (panel_order[q] % slab_count) * funcs, funcs, 2)
        for q in range(PANELS)
    ])
    (spread,) = gather("grp", 2, tiles)
    cols = jnp.stack([
        lax.dynamic_index_in_dim(spread, panel_order[q] // slab_count, 0, keepdims=False)[q]
        for q in range(PANELS)
    ])
    all_rows, all_cols = gather("blk", 3, reduced, cols)
    places_of = [slot_of(panel_order[q]) for q in range(PANELS)]
    upper = jnp.stack([lax.dynamic_index_in_dim(all_rows, p, 0, keepdims=False) for p in places_of])
    pivots = jnp.stack([lax.dynamic_index_in_dim(all_cols, p, 0, keepdims=False) for p in places_of])
    first, joint, second = pivot_inverses(pivots)
    schur = update(reduced, upper, cols, pivots[1, 0], first, joint, second)
    return (reduced, schur)


def solution(mesh):
    placed = (P(None, "blk", "grp", None), P(None, "blk", None, None), P(), P(), P())
    return jax.shard_map(
        on_device,
        mesh=mesh,
        in_specs=placed,
        out_specs=(P(None, "blk", "grp"), P(None, "blk", "grp")),
        check_vma=False,
    )
```

```python
import functools

import jax
import jax.numpy as jnp
from jax import lax
from jax.experimental import pallas as pl
from jax.experimental.pallas import tpu as pltpu
from jax.sharding import PartitionSpec as P

PANELS = 2

SELF_REAL = 12.0
SELF_IMAG = -3.0
COUPLE = 2.0
WAVE = 1.3

COS_TURN = (0.999999211770312, -19.738980419471126, 64.92865850463285, -85.27162830146948,
            58.79050662870376, -21.071108461771125)
SIN_TURN = (6.283184916984331, -41.34158926418157, 81.59994386455666, -76.61447586020026,
            41.342889428722025, -12.471244745942547)
TURNS = WAVE / (2.0 * 3.141592653589793)

HIGH = lax.Precision.HIGHEST


def horner(coefs, x):
    total = jnp.full_like(x, coefs[-1])
    for c in coefs[-2::-1]:
        total = total * x + c
    return total


def gather_kernel(axis, peers, count, *refs):
    sources, targets = refs[:count], refs[count:2 * count]
    send_sem, recv_sem, local_sem = refs[2 * count:]
    me = lax.axis_index(axis)
    barrier = pltpu.get_barrier_semaphore()
    for step in range(1, peers):
        pl.semaphore_signal(
            barrier, inc=1, device_id={axis: lax.rem(me + step, peers)}, device_id_type=pl.DeviceIdType.MESH
        )
    pl.semaphore_wait(barrier, peers - 1)

    def sent(which, step):
        return pltpu.make_async_remote_copy(
            src_ref=sources[which],
            dst_ref=targets[which].at[me],
            send_sem=send_sem.at[which, step - 1],
            recv_sem=recv_sem.at[which, step - 1],
            device_id={axis: lax.rem(me + step, peers)},
            device_id_type=pl.DeviceIdType.MESH,
        )

    copies = [sent(which, step) for step in range(1, peers) for which in range(count)]
    kept = [
        pltpu.make_async_copy(sources[which], targets[which].at[me], local_sem.at[which])
        for which in range(count)
    ]
    for copy in copies + kept:
        copy.start()
    for copy in kept + copies:
        copy.wait()


def gather(axis, collective_id, *values):
    peers = lax.axis_size(axis)
    count = len(values)
    anywhere = pl.BlockSpec(memory_space=pl.ANY)
    return pl.pallas_call(
        functools.partial(gather_kernel, axis, peers, count),
        in_specs=[anywhere] * count,
        out_specs=[anywhere] * count,
        out_shape=[jax.ShapeDtypeStruct((peers,) + v.shape, v.dtype) for v in values],
        scratch_shapes=[
            pltpu.SemaphoreType.DMA((count, peers - 1)),
            pltpu.SemaphoreType.DMA((count, peers - 1)),
            pltpu.SemaphoreType.DMA((count,)),
        ],
        compiler_params=pltpu.CompilerParams(collective_id=collective_id, has_side_effects=True),
        name="gather_" + axis + str(collective_id),
    )(*values)


def green_kernel(test_ref, basis_ref, out_ref):
    rows = out_ref.shape[1]
    unk = basis_ref.shape[2]
    chunk = 16

    def body(i, _):
        start = pl.multiple_of(i * chunk, chunk)
        test = test_ref[pl.ds(start, chunk), :]
        squared = None
        for which in range(3):
            spacing = test[:, which:which + 1] - basis_ref[0, which:which + 1, :]
            term = spacing * spacing
            squared = term if squared is None else squared + term
        coincide = squared == 0.0
        bounded = jnp.maximum(squared, 1.0)
        inverted = lax.rsqrt(bounded)
        turns = bounded * inverted * TURNS
        frac = turns - jnp.floor(turns + 0.5)
        frac2 = frac * frac
        scaled = COUPLE * inverted
        real = jnp.where(coincide, SELF_REAL, scaled * horner(COS_TURN, frac2))
        imag = jnp.where(coincide, SELF_IMAG, -(scaled * frac) * horner(SIN_TURN, frac2))
        out_ref[0, pl.ds(start, chunk), :unk] = real.astype(jnp.bfloat16)
        out_ref[0, pl.ds(start, chunk), unk:] = imag.astype(jnp.bfloat16)
        return 0

    lax.fori_loop(0, rows // chunk, body, 0)


def green_tiles(test_pos, basis_pos):
    unk = test_pos.shape[0]
    slab = basis_pos.shape[0]
    rows = min(256, unk)
    return pl.pallas_call(
        green_kernel,
        grid=(slab, unk // rows),
        in_specs=[
            pl.BlockSpec((rows, 3), lambda s, i: (i, 0)),
            pl.BlockSpec((1, 3, unk), lambda s, i: (s, 0, 0)),
        ],
        out_specs=pl.BlockSpec((1, rows, 2 * unk), lambda s, i: (s, i, 0)),
        out_shape=jax.ShapeDtypeStruct((slab, unk, 2 * unk), jnp.bfloat16),
        cost_estimate=pl.CostEstimate(
            flops=slab * unk * unk * 6000, bytes_accessed=slab * unk * unk * 4, transcendentals=slab * unk * unk
        ),
        name="green",
    )(test_pos, basis_pos)


def couple_kernel(green_ref, basis_ref, tested_ref, out_ref):
    real, imag = basis_ref[0, 0], basis_ref[1, 0]
    funcs = real.shape[1]
    top = jnp.concatenate([real, imag], axis=1)
    low = jnp.concatenate([-imag, real], axis=1)
    packed = jnp.concatenate([top, low], axis=0)
    product = jnp.dot(green_ref[0], packed, preferred_element_type=jnp.float32)
    high = product.astype(jnp.bfloat16)
    rest = (product - high.astype(jnp.float32)).astype(jnp.bfloat16)
    tested = tested_ref[...]
    outer = jnp.dot(tested, high, preferred_element_type=jnp.float32) + jnp.dot(
        tested, rest, preferred_element_type=jnp.float32
    )
    out_ref[0] = outer[:funcs, :funcs] + outer[funcs:, funcs:]
    out_ref[1] = outer[:funcs, funcs:] - outer[funcs:, :funcs]


def couple(green, slab_basis, tested):
    slab, unk, _ = green.shape
    funcs = slab_basis.shape[3]
    return pl.pallas_call(
        couple_kernel,
        grid=(slab,),
        in_specs=[
            pl.BlockSpec((1, unk, 2 * unk), lambda s: (s, 0, 0)),
            pl.BlockSpec((2, 1, unk, funcs), lambda s: (0, s, 0, 0)),
            pl.BlockSpec((2 * funcs, unk), lambda s: (0, 0)),
        ],
        out_specs=pl.BlockSpec((2, funcs, funcs), lambda s: (0, 0, s)),
        out_shape=jax.ShapeDtypeStruct((2, funcs, slab * funcs), jnp.float32),
        compiler_params=pltpu.CompilerParams(vmem_limit_bytes=40 * 1024 * 1024),
        cost_estimate=pl.CostEstimate(
            flops=slab * unk * unk * funcs * 8, bytes_accessed=slab * unk * unk * 4, transcendentals=0
        ),
        name="couple",
    )(green, slab_basis, tested)


def cdot(a, b):
    m, n = a[0].shape[0], b[0].shape[1]
    left = jnp.concatenate(a, axis=0)
    right = jnp.concatenate(b, axis=1)
    outer = jnp.dot(left, right, precision=HIGH, preferred_element_type=jnp.float32)
    return (outer[:m, :n] - outer[m:, n:], outer[:m, n:] + outer[m:, :n])


def csub(a, b):
    return (a[0] - b[0], a[1] - b[1])


def cadd(a, b):
    return (a[0] + b[0], a[1] + b[1])


def hermitian_inverse(herm):
    n = herm[0].shape[0]
    group = 8
    lane = lax.broadcasted_iota(jnp.int32, (1, n), 1)
    sub = lax.broadcasted_iota(jnp.int32, (group, 1), 0)

    def turn(_, carried):
        real, imag = carried
        head_r, head_i = real[:group], imag[:group]
        tail_r, tail_i = real[group:], imag[group:]
        for j in range(group):
            here = lane == j
            mine = sub == j
            row_r, row_i = head_r[j:j + 1, :], head_i[j:j + 1, :]
            scale = 1.0 / row_r[:, j:j + 1]
            row_r = jnp.where(here, 1.0, row_r) * scale
            row_i = jnp.where(here, 0.0, row_i) * scale
            col_r, col_i = tail_r[:, j:j + 1], tail_i[:, j:j + 1]
            tail_r = jnp.where(here, 0.0, tail_r) - col_r * row_r + col_i * row_i
            tail_i = jnp.where(here, 0.0, tail_i) - col_r * row_i - col_i * row_r
            col_r = jnp.where(mine, -1.0, head_r[:, j:j + 1])
            col_i = jnp.where(mine, 0.0, head_i[:, j:j + 1])
            gone = here | mine
            head_r = jnp.where(gone, 0.0, head_r) - col_r * row_r + col_i * row_i
            head_i = jnp.where(gone, 0.0, head_i) - col_r * row_i - col_i * row_r
        real = pltpu.roll(jnp.concatenate([tail_r, head_r], axis=0), n - group, 1)
        imag = pltpu.roll(jnp.concatenate([tail_i, head_i], axis=0), n - group, 1)
        return real, imag

    return lax.fori_loop(0, n // group, turn, herm)


def inverse_of(d):
    n = d[0].shape[0]
    adjoint = (d[0].T, -d[1].T)
    guess = cdot(hermitian_inverse(cdot(adjoint, d)), adjoint)
    off = cdot(d, guess)
    row = lax.broadcasted_iota(jnp.int32, (n, n), 0)
    col = lax.broadcasted_iota(jnp.int32, (n, n), 1)
    unit = jnp.where(row == col, 1.0, 0.0)
    return cadd(guess, cdot(guess, (unit - off[0], -off[1])))


def pivot_kernel(d_ref, first_ref, joint_ref, second_ref):
    def tile(i, j):
        return (d_ref[i, j, 0], d_ref[i, j, 1])

    first = inverse_of(tile(0, 0))
    joint = cdot(first, tile(0, 1))
    second = inverse_of(csub(tile(1, 1), cdot(tile(1, 0), joint)))
    for ref, value in ((first_ref, first), (joint_ref, joint), (second_ref, second)):
        ref[0] = value[0]
        ref[1] = value[1]


def pivot_inverses(pivots):
    funcs = pivots.shape[3]
    shape = jax.ShapeDtypeStruct((2, funcs, funcs), jnp.float32)
    return pl.pallas_call(
        pivot_kernel,
        out_shape=(shape, shape, shape),
        compiler_params=pltpu.CompilerParams(vmem_limit_bytes=32 * 1024 * 1024),
        cost_estimate=pl.CostEstimate(flops=20_000_000_000, bytes_accessed=1_000_000, transcendentals=0),
        name="pivots",
    )(pivots)


def update_kernel(full_ref, rows_ref, cols_ref, low_ref, first_ref, joint_ref, second_ref, out_ref):
    def pair(ref):
        return (ref[0], ref[1])

    upper0 = (rows_ref[0, 0], rows_ref[0, 1])
    upper1 = (rows_ref[1, 0], rows_ref[1, 1])
    begun = cdot(pair(first_ref), upper0)
    sol1 = cdot(pair(second_ref), csub(upper1, cdot(pair(low_ref), begun)))
    sol0 = csub(begun, cdot(pair(joint_ref), sol1))
    taken = cadd(
        cdot((cols_ref[0, 0], cols_ref[0, 1]), sol0), cdot((cols_ref[1, 0], cols_ref[1, 1]), sol1)
    )
    out_ref[0] = full_ref[0] - taken[0]
    out_ref[1] = full_ref[1] - taken[1]


def update(full, rows, cols, low, first, joint, second):
    return pl.pallas_call(
        update_kernel,
        out_shape=jax.ShapeDtypeStruct(full.shape, jnp.float32),
        compiler_params=pltpu.CompilerParams(vmem_limit_bytes=32 * 1024 * 1024),
        cost_estimate=pl.CostEstimate(flops=2_000_000_000, bytes_accessed=2_000_000, transcendentals=0),
        name="update",
    )(full, rows, cols, low, first, joint, second)


def on_device(inverse, excite, coordinates, block_of_slot, panel_order):
    funcs = excite.shape[3]
    blocks = block_of_slot.shape[0]
    grp_index = lax.axis_index("grp")
    slab_count = blocks // lax.axis_size("grp")
    own_id = block_of_slot[lax.axis_index("blk")]

    exc_r, exc_i = excite[0, 0], excite[1, 0]
    right_r = jnp.concatenate([exc_r, exc_i], axis=1)
    right_i = jnp.concatenate([-exc_i, exc_r], axis=1)
    rows = jnp.dot(inverse[0, 0], right_r, preferred_element_type=jnp.float32) + jnp.dot(
        inverse[1, 0], right_i, preferred_element_type=jnp.float32
    )
    basis_rows = jnp.stack([rows[:, :funcs], rows[:, funcs:]]).astype(jnp.bfloat16)

    places = coordinates.astype(jnp.float32)
    own_pos = lax.dynamic_index_in_dim(places, own_id, 1, keepdims=False).T
    slab_pos = lax.dynamic_slice_in_dim(places, grp_index * slab_count, slab_count, 1)
    green = green_tiles(own_pos, jnp.transpose(slab_pos, (1, 0, 2)))

    (whole,) = gather("grp", 1, basis_rows)
    whole, basis_rows = lax.optimization_barrier((whole, basis_rows))
    (sliced,) = gather("blk", 0, basis_rows)
    slots = jnp.arange(blocks, dtype=jnp.int32)

    def slot_of(block):
        return jnp.sum(jnp.where(block_of_slot == block, slots, 0))

    chosen = (block_of_slot[None, :] == slots[:, None])[:, :, None, None, None]
    grouped = jnp.sum(jnp.where(chosen, sliced[None], 0), axis=1, dtype=jnp.float32).astype(jnp.bfloat16)
    slab = lax.all_to_all(grouped, "grp", split_axis=0, concat_axis=2, tiled=True)
    slab = jnp.transpose(slab, (1, 0, 2, 3))
    tested = jnp.transpose(whole, (1, 3, 0, 2)).reshape(2 * funcs, -1)

    reduced = couple(green, slab, tested)
    all_rows = lax.all_gather(reduced, "blk")

    tiles = jnp.stack([
        lax.dynamic_slice_in_dim(reduced, (panel_order[q] % slab_count) * funcs, funcs, 2)
        for q in range(PANELS)
    ])
    (spread,) = gather("grp", 2, tiles)
    cols = jnp.stack([
        lax.dynamic_index_in_dim(spread, panel_order[q] // slab_count, 0, keepdims=False)[q]
        for q in range(PANELS)
    ])
    (all_cols,) = gather("blk", 3, cols)
    places_of = [slot_of(panel_order[q]) for q in range(PANELS)]
    upper = jnp.stack([lax.dynamic_index_in_dim(all_rows, p, 0, keepdims=False) for p in places_of])
    pivots = jnp.stack([lax.dynamic_index_in_dim(all_cols, p, 0, keepdims=False) for p in places_of])
    first, joint, second = pivot_inverses(pivots)
    schur = update(reduced, upper, cols, pivots[1, 0], first, joint, second)
    return (reduced, schur)


def solution(mesh):
    placed = (P(None, "blk", "grp", None), P(None, "blk", None, None), P(), P(), P())
    return jax.shard_map(
        on_device,
        mesh=mesh,
        in_specs=placed,
        out_specs=(P(None, "blk", "grp"), P(None, "blk", "grp")),
        check_vma=False,
    )
```
